512 devices in a mesh: leaf: 16 (over y, z_lo), panel: 32 (over z_hi, x, core).
Axes of the slice: x: 4, y: 8, z: 8 (z_hi: 4, z_lo: 2; z = z_hi * 2 + z_lo), core: 2. Of those that a mesh axis runs over, the one named last changes fastest.
Arguments:
- child_stiff: bfloat16 [16, 4096, 4096], P('leaf', None, 'panel'), may hold values from -4 to 4
- child_bound: bfloat16 [16, 4096, 2048], P('leaf', 'panel'), may hold values from -6 to 6
- child_modes: bfloat16 [16, 2048, 512], P('leaf'), may hold values from -0.125 to 0.125
- child_inv_eig: float32 [16, 512], P('leaf'), may hold values from 0.005 to 0.1
- child_map: int32 [16, 32], P('leaf'), may hold values from 0 to 31
- parent_bound: bfloat16 [16, 4096, 2048], P('leaf', 'panel'), may hold values from -6 to 6
- parent_modes: bfloat16 [16, 2048, 256], P('leaf'), may hold values from -0.125 to 0.125
- parent_inv_eig: float32 [16, 256], P('leaf'), may hold values from 0.005 to 0.1
- parent_map: int32 [8, 32], replicated, may hold values from 0 to 31
- interface_basis: bfloat16 [16, 4096, 256], P('leaf', 'panel'), may hold values from -0.09375 to 0.09375
Outputs:
- reduced: float32 [16, 256, 1024], P('leaf', 'panel')
The draws below stay inside these ranges and needn't reach their ends.
Inputs may be any that keep to these rules, and one draw needn't show every extreme that they name: `child_map`: each entry names a panel of the section below. `parent_map`: each entry names a panel of the parent section.
All inputs are finite; a program needn't handle non-finite values.
Results may differ from the reference program's by a relative error of at most 0.023.
Values may be sent and summed in bfloat16 or wider, within the bound.
No kernel may reach another device: no remote copies, remote signals or barrier semaphores. Data moves between devices by JAX's collectives and lax.ppermute only.
A program may use at most 128 MiB of HBM per device.

```python
import math
import jax
import jax.numpy as jnp
from jax import lax

B = 4096
M = 512
MH = 256
NI = 2048
R = 1024
RQ = 256
NP = 32
LEAVES = 16
PARENTS = 8


def set_ends(values, key, smallest, top_value):
    longest = values.shape.index(max(values.shape))
    spots = []
    for shift in (0, 1):
        where = [jax.random.randint(jax.random.fold_in(key, axis), (), 0, length) for axis, length in enumerate(values.shape)]
        where[longest] = (where[longest] + shift) % values.shape[longest]
        spots.append(tuple(where))
    return values.at[spots[0]].set(smallest).at[spots[1]].set(top_value)


def steps_of(stream_key, dims, cuts, least, high):
    def one(dim, parts):
        steps = jax.random.uniform(jax.random.fold_in(jax.random.fold_in(stream_key, 6), dim), (parts,), jnp.float32, least / len(cuts), high / len(cuts))
        return jnp.repeat(jnp.exp(steps), dims[dim] // parts).reshape((-1,) + (1,) * (len(dims) - dim - 1))

    loudness = one(*cuts[0])
    for cut in cuts[1:]:
        loudness = loudness * one(*cut)
    return loudness


def scatter_about(rng, shape, scale, most, shards=(), kind=jnp.bfloat16):
    values = jax.random.normal(rng, shape, jnp.float32) * scale
    if len(shards) > 0:
        values = steps_of(rng, shape, shards, -0.22, 0.18) * values
    return jnp.clip(values, min=-most, max=most).astype(kind)


def setup_inputs(seed: int = 0) -> dict:
    arg_keys = jax.random.split(jax.random.key(seed), 11)
    return {
        "child_stiff": scatter_about(arg_keys[0], (LEAVES, B, B), 0.5, 4.0, ((0, 16), (2, 32))),
        "child_bound": scatter_about(arg_keys[1], (LEAVES, B, NI), 1.0, 6.0, ((0, 16), (1, 32))),
        "child_modes": scatter_about(arg_keys[2], (LEAVES, NI, M), NI ** -0.5, 0.125, ((0, 16),)),
        "child_inv_eig": jnp.clip(jnp.exp(math.log(0.1) - 2.9957323 * jax.random.uniform(arg_keys[3], (LEAVES, M), jnp.float32) ** steps_of(arg_keys[3], (LEAVES, M), ((0, 16),), -0.2, 0.2)), 0.005, 0.1),
        "child_map": set_ends(jax.random.randint(arg_keys[4], (LEAVES, NP), 0, NP), jax.random.fold_in(arg_keys[4], 1), 0, NP - 1).astype(jnp.int32),
        "parent_bound": scatter_about(arg_keys[5], (LEAVES, B, NI), 1.0, 6.0, ((0, 16), (1, 32))),
        "parent_modes": scatter_about(arg_keys[6], (LEAVES, NI, MH), NI ** -0.5, 0.125, ((0, 16),)),
        "parent_inv_eig": jnp.clip(jnp.exp(math.log(0.1) - 2.9957323 * jax.random.uniform(arg_keys[7], (LEAVES, MH), jnp.float32) ** steps_of(arg_keys[7], (LEAVES, MH), ((0, 16),), -0.2, 0.2)), 0.005, 0.1),
        "parent_map": set_ends(jax.random.randint(arg_keys[8], (PARENTS, NP), 0, NP), jax.random.fold_in(arg_keys[8], 1), 0, NP - 1).astype(jnp.int32),
        "interface_basis": scatter_about(arg_keys[9], (LEAVES, B, RQ), B ** -0.5, 0.09375, ((0, 16), (1, 32))),
    }


def regroup(matrix, panel_index):
    panels = panel_index.shape[0]
    stacked = matrix.reshape(panels, matrix.shape[0] // panels, matrix.shape[1])
    return jnp.take(stacked, panel_index, axis=0).reshape(matrix.shape)


def project_pair(bound_rows, basis_modes, inv_eig):
    coupling = jnp.dot(bound_rows, basis_modes, preferred_element_type=jnp.float32).astype(jnp.bfloat16)
    scaled = (coupling.astype(jnp.float32) * inv_eig[None, :]).astype(jnp.bfloat16)
    return coupling, scaled


def outer_term(coupling, scaled):
    return jnp.dot(coupling, scaled.T, preferred_element_type=jnp.float32)


def one_grand(bundle):
    (stiffness, child_bound, child_modes, child_inv_eig, child_map,
     parent_bound, parent_modes, parent_inv_eig, parent_map, interface_basis) = bundle
    regrouped = []
    for parent_slot in range(2):
        assembled = jnp.zeros((B, B), jnp.float32)
        correction = jnp.zeros((B, B), jnp.float32)
        for child_slot in range(2):
            leaf_slot = 2 * parent_slot + child_slot
            coupling, scaled = project_pair(child_bound[leaf_slot], child_modes[leaf_slot], child_inv_eig[leaf_slot])
            schur_block = stiffness[leaf_slot].astype(jnp.float32) - outer_term(coupling, scaled)
            assembled = assembled + regroup(schur_block, child_map[leaf_slot])
            parent_coupling, parent_scaled = project_pair(parent_bound[leaf_slot], parent_modes[leaf_slot], parent_inv_eig[leaf_slot])
            correction = correction + outer_term(parent_coupling, parent_scaled)
        regrouped.append(regroup(assembled - correction, parent_map[parent_slot]))
    grand = (regrouped[0] + regrouped[1]).astype(jnp.bfloat16)
    whole_basis = jnp.concatenate([interface_basis[quarter] for quarter in range(4)], axis=1)
    results = []
    for quarter in range(4):
        projected = jnp.dot(interface_basis[quarter].T, grand, preferred_element_type=jnp.float32).astype(jnp.bfloat16)
        results.append(jnp.dot(projected, whole_basis, preferred_element_type=jnp.float32))
    return jnp.stack(results)


def reference(child_stiff, child_bound, child_modes, child_inv_eig, child_map, parent_bound, parent_modes, parent_inv_eig, parent_map, interface_basis):
    groups = LEAVES // 4

    def by_group(array):
        return array.reshape((groups, 4) + array.shape[1:])

    bundle = (by_group(child_stiff), by_group(child_bound), by_group(child_modes), by_group(child_inv_eig),
              by_group(child_map), by_group(parent_bound), by_group(parent_modes), by_group(parent_inv_eig),
              parent_map.reshape(groups, 2, parent_map.shape[1]), by_group(interface_basis))
    reduced = lax.map(one_grand, bundle)
    return reduced.reshape(LEAVES, RQ, R)
```

```python
import jax
import jax.numpy as jnp
from jax import lax
from jax.sharding import Mesh
from jax.sharding import PartitionSpec as P

LEAF = ("b", "a")
PANEL = ("z", "x", "c")
GROUP = LEAF + PANEL
F32 = jnp.float32
BF16 = jnp.bfloat16


def exchange(value, axis):
    return lax.all_to_all(value, axis, 0, 0, tiled=True)


def spread(value, axis, count):
    return exchange(jnp.broadcast_to(value[None], (count,) + value.shape), axis)


def shards(
    child_stiff,
    child_bound,
    child_modes,
    child_inv_eig,
    child_map,
    parent_bound,
    parent_modes,
    parent_inv_eig,
    parent_map,
    interface_basis,
):
    panel = lax.axis_index(PANEL)
    core = lax.axis_index("c")
    grand_index = lax.axis_index("g")
    own_basis = interface_basis[0]
    width = own_basis.shape[1]
    pair_maps = lax.dynamic_slice_in_dim(parent_map, 2 * grand_index, 2, 0)
    leaf_maps = jnp.repeat(pair_maps, 2, axis=0)

    def coupling(modes, bound):
        return lax.dot_general(
            modes, bound, (((0,), (1,)), ((), ())), preferred_element_type=F32
        ).astype(BF16)

    child_t = coupling(child_modes[0], child_bound[0]).reshape(32, 16, 128)
    parent_t = coupling(parent_modes[0], parent_bound[0]).reshape(32, 8, 128)
    modes_t = jnp.concatenate([child_t, parent_t], axis=1)
    columns = exchange(jnp.broadcast_to(modes_t[None], (4, 32, 24, 128)).reshape(128, 24, 128), GROUP)
    columns = columns.reshape(4, 32, 24, 128)

    basis = spread(own_basis, "z", 4).reshape(4, 128, width)
    basis = spread(basis, "x", 4).reshape(4, 4, 128, width)
    other = lax.ppermute(basis, "c", [(0, 1), (1, 0)])
    both = jnp.where(core == 0, jnp.stack([basis, other]), jnp.stack([other, basis]))
    basis_all = both.transpose(2, 1, 0, 3, 4).reshape(32, 128, width)

    eig = jnp.concatenate([child_inv_eig[0], parent_inv_eig[0]]).reshape(3, width)
    eig_hi = eig.astype(BF16)
    eig_lo = (eig - eig_hi.astype(F32)).astype(BF16)
    map_row = jnp.pad(child_map.astype(BF16), ((0, 0), (0, width - child_map.shape[1])))
    extra = jnp.concatenate([eig_hi, eig_lo, map_row, jnp.zeros((9, width), BF16)], axis=0)
    quad = spread(jnp.concatenate([own_basis, extra], axis=0), LEAF, 4).reshape(4, 144, width)
    panel_basis = quad[:, :128]
    eigs = (quad[:, 128:131].astype(F32) + quad[:, 131:134].astype(F32)).reshape(4, 768)
    eigs = jnp.concatenate(
        [
            lax.dynamic_slice_in_dim(eigs, 16 * panel, 16, 1),
            lax.dynamic_slice_in_dim(eigs, 512 + 8 * panel, 8, 1),
        ],
        axis=1,
    )
    child_maps = quad[:, 134, :32].astype(jnp.int32)

    own_pmap = lax.dynamic_index_in_dim(pair_maps, lax.axis_index("b"), 0, keepdims=False)
    rows = child_map[0].at[own_pmap].get(mode="promise_in_bounds")
    stiff = child_stiff[0].reshape(32, 128, 128).at[rows].get(mode="promise_in_bounds")
    parts = exchange(stiff.reshape(4, 1024, 128), LEAF)
    summed = jnp.sum(parts.astype(F32), axis=0).astype(BF16)
    assembled = spread(summed, LEAF, 4).reshape(32, 128, 128)

    right = jnp.einsum("ljmr,jrc->lmc", columns, basis_all, preferred_element_type=F32)
    right = (-eigs[:, :, None] * right).astype(BF16).reshape(96, width)
    right = spread(right, LEAF, 4).reshape(4, 96, width)

    child_rows = jnp.take_along_axis(child_maps, leaf_maps, axis=1)
    take = jax.vmap(lambda part, index: part.at[index].get(mode="promise_in_bounds"))
    regrouped = jnp.concatenate(
        [take(columns[:, :, :16], child_rows), take(columns[:, :, 16:], leaf_maps)], axis=2
    )
    left = jnp.einsum("limr,irc->lmc", regrouped, basis_all, preferred_element_type=F32)
    left = left.astype(BF16).reshape(96, width)
    left_stiff = jnp.einsum("irk,irc->kc", assembled, basis_all, preferred_element_type=F32).astype(BF16)

    part = jnp.einsum("kc,qkd->cqd", left_stiff, panel_basis, preferred_element_type=F32)
    part = part + jnp.einsum("kc,qkd->cqd", left, right, preferred_element_type=F32)
    part = part.reshape(16, 2, 8, 1024)
    mine = lax.dynamic_index_in_dim(part, core, 1, keepdims=False)
    theirs = lax.dynamic_index_in_dim(part, 1 - core, 1, keepdims=False).astype(BF16)
    mine = mine + lax.ppermute(theirs, "c", [(0, 1), (1, 0)]).astype(F32)
    pieces = exchange(mine.astype(BF16), ("z", "x"))
    return jnp.sum(pieces.astype(F32), axis=0)[None]


def solution(mesh):
    names = ("g", "b", "a", "z", "x", "c")
    split = Mesh(mesh.devices.reshape(4, 2, 2, 4, 4, 2), names)
    leaf = ("g", "b", "a")
    placed = (
        P(leaf, None, PANEL),
        P(leaf, PANEL, None),
        P(leaf, None, None),
        P(leaf, None),
        P(leaf, None),
        P(leaf, PANEL, None),
        P(leaf, None, None),
        P(leaf, None),
        P(),
        P(leaf, PANEL, None),
    )
    return jax.shard_map(
        shards, mesh=split, in_specs=placed, out_specs=P(leaf, PANEL, None), check_vma=False
    )
```

```python
import functools

import jax
import jax.numpy as jnp
from jax import lax
from jax.experimental import pallas as pl
from jax.experimental.pallas import tpu as pltpu
from jax.sharding import Mesh
from jax.sharding import PartitionSpec as P

PANEL = ("z", "x", "c")
GROUP = ("b", "a") + PANEL
F32 = jnp.float32
BF16 = jnp.bfloat16
VM = pl.BlockSpec(memory_space=pltpu.VMEM)
SM = pl.BlockSpec(memory_space=pltpu.SMEM)


def call(body, outs, specs, name, flops, *args):
    shapes = [jax.ShapeDtypeStruct(s, t) for s, t in outs]
    moved = sum(a.size * a.dtype.itemsize for a in args)
    return pl.pallas_call(
        body,
        out_shape=shapes,
        in_specs=specs,
        out_specs=[VM] * len(outs),
        compiler_params=pltpu.CompilerParams(vmem_limit_bytes=32 << 20),
        cost_estimate=pl.CostEstimate(flops=flops, bytes_accessed=moved, transcendentals=0),
        name=name,
    )(*args)


def dot(left, right):
    return jnp.dot(left, right, preferred_element_type=F32)


def coupling_body(cm_ref, cb_ref, ce_ref, pm_ref, pb_ref, pe_ref, out_ref, child_ref, parent_ref):
    step = pl.program_id(0)

    @pl.when(step == 0)
    def _():
        child_ref[...] = jnp.zeros_like(child_ref)
        parent_ref[...] = jnp.zeros_like(parent_ref)

    child_ref[...] += dot(cb_ref[...], cm_ref[...])
    parent_ref[...] += dot(pb_ref[...], pm_ref[...])

    @pl.when(step == pl.num_programs(0) - 1)
    def _():
        child = child_ref[...] * jnp.sqrt(ce_ref[...])
        parent = parent_ref[...] * jnp.sqrt(pe_ref[...])
        both = jnp.concatenate(
            [child.T.reshape(32, 16, 128), parent.T.reshape(32, 8, 128)], axis=1
        ).astype(BF16)
        for q in range(4):
            out_ref[q] = both


def couple(child_modes, child_bound, child_eig, parent_modes, parent_bound, parent_eig):
    steps = 4
    depth = child_modes.shape[0] // steps
    modes = lambda width: pl.BlockSpec((depth, width), lambda i: (i, 0))
    bound = pl.BlockSpec((128, depth), lambda i: (0, i))
    eig = lambda width: pl.BlockSpec((1, width), lambda i: (0, 0))
    return pl.pallas_call(
        coupling_body,
        grid=(steps,),
        out_shape=jax.ShapeDtypeStruct((4, 32, 24, 128), BF16),
        in_specs=[modes(512), bound, eig(512), modes(256), bound, eig(256)],
        out_specs=pl.BlockSpec((4, 32, 24, 128), lambda i: (0, 0, 0, 0)),
        scratch_shapes=[pltpu.VMEM((128, 512), F32), pltpu.VMEM((128, 256), F32)],
        compiler_params=pltpu.CompilerParams(vmem_limit_bytes=60 << 20),
        cost_estimate=pl.CostEstimate(flops=400_000_000, bytes_accessed=5_000_000, transcendentals=0),
        name="coupling",
    )(child_modes, child_bound, child_eig, parent_modes, parent_bound, parent_eig)


def join_body(a_ref, b_ref, c_ref, d_ref, out_ref):
    for k, ref in enumerate((a_ref, b_ref, c_ref, d_ref)):
        out_ref[512 * k : 512 * (k + 1), :] = ref[...]


def stiff_body(stiff_ref, cmap_ref, pmap_ref, row_ref, basis_ref, out_ref):
    def place(i, carry):
        row = cmap_ref[0, pmap_ref[0, i]]
        out_ref[pl.ds(pl.multiple_of(i * 128, 128), 128), :] = stiff_ref[
            pl.ds(pl.multiple_of(row * 128, 128), 128), :
        ]
        return carry

    lax.fori_loop(0, 32, place, 0)
    out_ref[4096:4224, :] = basis_ref[:, :128]
    out_ref[4224:4352, :] = basis_ref[:, 128:]
    row = jnp.concatenate([row_ref[...], jnp.zeros((1, 96), jnp.int32)], axis=1).astype(F32)
    out_ref[4352:4368, :] = jnp.broadcast_to(row, (16, 128)).astype(BF16)


def add_body(own_ref, got_ref, out_ref):
    def add(i, carry):
        at = pl.ds(pl.multiple_of(i * 512, 512), 512)
        out_ref[at, :] = (own_ref[at, :].astype(F32) + got_ref[at, :].astype(F32)).astype(BF16)
        return carry

    lax.fori_loop(0, 8, add, 0)
    out_ref[4096:4368, :] = own_ref[4096:, :]
    out_ref[4368:, :] = got_ref[4096:, :]


def block_index(pos_ref, half, k):
    return (k % 4) * 8 + (pos_ref[0] ^ (k // 4)) * 2 + (pos_ref[1] ^ half)


def right_body(pos_ref, col_ref, mine_ref, other_ref, out_ref):
    total = jnp.zeros((96, 256), F32)
    for half, ref in enumerate((mine_ref, other_ref)):
        for k in range(0, 16, 2):
            cols = [
                col_ref[:, block_index(pos_ref, half, k + s)].astype(F32).reshape(96, 128)
                for s in (0, 1)
            ]
            left = jnp.concatenate(cols, axis=1).astype(BF16)
            total = total + dot(left, ref[pl.ds(k * 128, 256), :])
    total = total.astype(BF16)
    for q in range(4):
        out_ref[q] = total


def left_body(pos_ref, cmaps_ref, pmaps_ref, col_ref, mine_ref, other_ref, own_ref, far_ref, out_ref):
    modes = jnp.zeros((96, 256), F32)
    stiff = jnp.zeros((128, 256), F32)
    q = pos_ref[2]
    for half, ref in enumerate((mine_ref, other_ref)):
        for k in range(0, 16, 2):
            pair, rows = [], []
            for s in (0, 1):
                i = block_index(pos_ref, half, k + s)
                for_leaf = []
                for leaf in range(4):
                    row = pmaps_ref[leaf // 2, i]
                    for_leaf.append(col_ref[leaf, cmaps_ref[leaf ^ q, row]].astype(F32)[:16])
                    for_leaf.append(col_ref[leaf, row].astype(F32)[16:])
                pair.append(jnp.concatenate(for_leaf, axis=0))
                at = pl.ds(pl.multiple_of(i * 128, 128), 128)
                rows.append((own_ref[at, :].astype(F32) + far_ref[at, :].astype(F32)).T)
            block = ref[pl.ds(k * 128, 256), :]
            modes = modes + dot(jnp.concatenate(pair, axis=1).astype(BF16), block)
            stiff = stiff + dot(jnp.concatenate(rows, axis=1).astype(BF16), block)
    out_ref[:128, :] = stiff
    out_ref[128:, :] = -modes


def final_body(pos_ref, left_ref, right_ref, w0_ref, w1_ref, mine_ref, theirs_ref, all_ref):
    left = left_ref[...].T.astype(BF16)
    q = pos_ref[2]
    for rel in range(4):
        at = q ^ rel
        w_ref = (w0_ref, w1_ref)[rel % 2]
        base = 272 * (rel // 2) + 4096
        basis = jnp.concatenate([w_ref[base : base + 128, :], w_ref[base + 128 : base + 256, :]], axis=1)
        stacked = jnp.concatenate([basis.astype(F32), right_ref[at].astype(F32)], axis=0).astype(BF16)
        all_ref[:, pl.ds(pl.multiple_of(at * 256, 256), 256)] = dot(left, stacked)
    c = pos_ref[1]
    mine, theirs = [], []
    for t in range(16):
        mine.append(all_ref[pl.ds(pl.multiple_of(16 * t + 8 * c, 8), 8), :])
        theirs.append(all_ref[pl.ds(pl.multiple_of(16 * t + 8 * (1 - c), 8), 8), :])
    mine_ref[...] = jnp.concatenate(mine, axis=0)
    theirs_ref[...] = jnp.concatenate(theirs, axis=0).astype(BF16)


def swap(value, axis, mask):
    size = lax.axis_size(axis)
    return lax.ppermute(value, axis, [(i, i ^ mask) for i in range(size)])


def exchange(value, axis):
    return lax.all_to_all(value, axis, 0, 0, tiled=True)


def shards(
    child_stiff,
    child_bound,
    child_modes,
    child_inv_eig,
    child_map,
    parent_bound,
    parent_modes,
    parent_inv_eig,
    parent_map,
    interface_basis,
):
    quad_place = 2 * lax.axis_index("b") + lax.axis_index("a")
    pos = jnp.stack([lax.axis_index("x"), lax.axis_index("c"), quad_place])
    own_basis = interface_basis[0]
    pair_maps = lax.dynamic_slice_in_dim(parent_map, 2 * lax.axis_index("g"), 2, 0)
    own_pmap = lax.dynamic_slice_in_dim(pair_maps, lax.axis_index("b"), 1, 0)

    modes_t = couple(
        child_modes[0], child_bound[0], child_inv_eig, parent_modes[0], parent_bound[0], parent_inv_eig
    )
    columns = exchange(modes_t.reshape(128, 24, 128), GROUP).reshape(4, 32, 24, 128)

    by_z = exchange(jnp.broadcast_to(own_basis[None], (4, 128, 256)), "z").reshape(512, 256)
    (mine,) = call(
        join_body, [((2048, 256), BF16)], [VM] * 4, "join", 1_000_000,
        by_z, *[swap(by_z, "x", d) for d in (1, 2, 3)],
    )
    other = swap(mine, "c", 1)

    (stiff,) = call(
        stiff_body, [((4368, 128), BF16)], [VM, SM, SM, VM, VM], "regroup", 1_000_000,
        child_stiff[0], child_map, own_pmap, child_map, own_basis,
    )
    (near,) = call(add_body, [((4640, 128), BF16)], [VM] * 2, "add", 1_000_000, stiff, swap(stiff, "b", 1))
    far = swap(near, "a", 1)

    (right,) = call(
        right_body, [((4, 96, 256), BF16)], [SM, VM, VM, VM], "right", 200_000_000, pos, columns, mine, other
    )
    child_maps = jnp.stack(
        [near[4352, :32], far[4352, :32], near[4624, :32], far[4624, :32]]
    ).astype(jnp.int32)
    right = exchange(right.reshape(384, 256), ("b", "a")).reshape(4, 96, 256)
    (left,) = call(
        left_body, [((224, 256), F32)], [SM, SM, SM] + [VM] * 5, "left", 500_000_000,
        pos, child_maps, pair_maps, columns, mine, other, near, far,
    )
    kept, sent = pl.pallas_call(
        final_body,
        out_shape=[jax.ShapeDtypeStruct((128, 1024), F32), jax.ShapeDtypeStruct((128, 1024), BF16)],
        in_specs=[SM] + [VM] * 4,
        out_specs=[VM, VM],
        scratch_shapes=[pltpu.VMEM((256, 1024), F32)],
        compiler_params=pltpu.CompilerParams(vmem_limit_bytes=32 << 20),
        cost_estimate=pl.CostEstimate(flops=120_000_000, bytes_accessed=2_000_000, transcendentals=0),
        name="product",
    )(pos, left, right, near, far)
    total = (kept + swap(sent, "c", 1).astype(F32)).astype(BF16)
    pieces = exchange(total.reshape(16, 8, 1024), ("z", "x"))
    return jnp.sum(pieces.astype(F32), axis=0)[None]


def solution(mesh):
    names = ("g", "b", "a", "z", "x", "c")
    split = Mesh(mesh.devices.reshape(4, 2, 2, 4, 4, 2), names)
    leaf = ("g", "b", "a")
    placed = (
        P(leaf, None, PANEL),
        P(leaf, PANEL, None),
        P(leaf, None, None),
        P(leaf, None),
        P(leaf, None),
        P(leaf, PANEL, None),
        P(leaf, None, None),
        P(leaf, None),
        P(),
        P(leaf, PANEL, None),
    )
    return jax.shard_map(
        shards, mesh=split, in_specs=placed, out_specs=P(leaf, PANEL, None), check_vma=False
    )
```

```python
import functools

import jax
import jax.numpy as jnp
from jax import lax
from jax.experimental import pallas as pl
from jax.experimental.pallas import tpu as pltpu
from jax.sharding import Mesh
from jax.sharding import PartitionSpec as P

PANEL = ("z", "x", "c")
LEAF = ("b", "a")
F32 = jnp.float32
BF16 = jnp.bfloat16
VM = pl.BlockSpec(memory_space=pltpu.VMEM)
SM = pl.BlockSpec(memory_space=pltpu.SMEM)
ANY = pl.BlockSpec(memory_space=pl.ANY)


def call(body, outs, specs, name, flops, *args):
    shapes = [jax.ShapeDtypeStruct(s, t) for s, t in outs]
    moved = sum(a.size * a.dtype.itemsize for a in args)
    return pl.pallas_call(
        body,
        out_shape=shapes,
        in_specs=specs,
        out_specs=[VM] * len(outs),
        compiler_params=pltpu.CompilerParams(vmem_limit_bytes=12 << 20),
        cost_estimate=pl.CostEstimate(flops=0, bytes_accessed=0, transcendentals=0),
        name=name,
    )(*args)


def dot(left, right):
    return jnp.dot(left, right, preferred_element_type=F32)


def coupling_body(
    cm_ref, cb_ref, ce_ref, pm_ref, pb_ref, pe_ref, u_ref, out_ref, child_ref, parent_ref
):
    step = pl.program_id(0)

    @pl.when(step == 0)
    def _():
        child_ref[...] = jnp.zeros_like(child_ref)
        parent_ref[...] = jnp.zeros_like(parent_ref)

    child_ref[...] += dot(cb_ref[...], cm_ref[...])
    parent_ref[...] += dot(pb_ref[...], pm_ref[...])

    @pl.when(step == pl.num_programs(0) - 1)
    def _():
        child = child_ref[...] * jnp.sqrt(ce_ref[...])
        parent = parent_ref[...] * jnp.sqrt(pe_ref[...])
        both = jnp.concatenate(
            [child.T.reshape(32, 16, 128), parent.T.reshape(32, 8, 128)], axis=1
        ).reshape(768, 128).astype(BF16)
        for z in range(4):
            out_ref[z, :192, :] = both[192 * z : 192 * (z + 1)]
            out_ref[z, 192:320, :] = u_ref[:, :128]
            out_ref[z, 320:, :] = u_ref[:, 128:]


def couple(*args):
    steps = 2
    depth = args[0].shape[0] // steps
    modes = lambda width: pl.BlockSpec((depth, width), lambda i: (i, 0))
    bound = pl.BlockSpec((128, depth), lambda i: (0, i))
    whole = lambda *shape: pl.BlockSpec(shape, lambda i: (0,) * len(shape))
    return pl.pallas_call(
        coupling_body,
        grid=(steps,),
        out_shape=jax.ShapeDtypeStruct((4, 448, 128), BF16),
        in_specs=[modes(512), bound, whole(1, 512), modes(256), bound, whole(1, 256), whole(128, 256)],
        out_specs=whole(4, 448, 128),
        scratch_shapes=[pltpu.VMEM((128, 512), F32), pltpu.VMEM((128, 256), F32)],
        compiler_params=pltpu.CompilerParams(vmem_limit_bytes=60 << 20),
        cost_estimate=pl.CostEstimate(flops=0, bytes_accessed=0, transcendentals=0),
        name="coupling",
    )(*args)


def regroup_body(stiff_ref, cmap_ref, pmap_ref, keep_ref, send_ref, sems):
    b = lax.axis_index("b")
    parent = 2 * lax.axis_index("g") + b
    for i in range(16):
        for k, (ref, half) in enumerate(((keep_ref, b), (send_ref, 1 - b))):
            row = cmap_ref[0, pmap_ref[parent, half * 16 + i]]
            pltpu.make_async_copy(
                stiff_ref.at[pl.ds(pl.multiple_of(row * 128, 128), 128)], ref.at[pl.ds(i * 128, 128)], sems.at[k]
            ).start()
    for k, ref in enumerate((keep_ref, send_ref)):
        pltpu.make_async_copy(stiff_ref.at[pl.ds(0, 2048)], ref, sems.at[k]).wait()


def regroup(*args):
    return pl.pallas_call(
        regroup_body,
        out_shape=[jax.ShapeDtypeStruct((2048, 128), BF16)] * 2,
        in_specs=[ANY, SM, SM],
        out_specs=[VM, VM],
        scratch_shapes=[pltpu.SemaphoreType.DMA((2,))],
        compiler_params=pltpu.CompilerParams(vmem_limit_bytes=12 << 20),
        cost_estimate=pl.CostEstimate(flops=0, bytes_accessed=0, transcendentals=0),
        name="regroup",
    )(*args)


def split_body(got_ref, out_ref):
    parts = [got_ref[z, :192, :].astype(F32).reshape(8, 24, 128) for z in range(4)]
    columns = jnp.concatenate(parts, axis=1).astype(BF16)
    for k in range(8):
        out_ref[k, :96, :] = columns[k]
        for z in range(4):
            at = 192 + 128 * (k % 2)
            out_ref[k, 96 + 128 * z : 224 + 128 * z, :] = got_ref[z, at : at + 128, :]


def repeat_body(one_ref, basis_ref, row_ref, near_ref, far_ref, out_ref, half_ref):
    half_ref[...] = (near_ref[...].astype(F32) + far_ref[...].astype(F32)).astype(BF16)
    row = jnp.concatenate([row_ref[...], jnp.zeros((1, 96), jnp.int32)], axis=1).astype(F32)
    basis = basis_ref[...].astype(F32)
    rest = jnp.concatenate([basis[:, :128], basis[:, 128:], jnp.broadcast_to(row, (32, 128))], axis=0)
    rest = rest.reshape(12, 24, 128).astype(BF16)
    columns = one_ref[:, :96, :].astype(F32).reshape(32, 24, 128).astype(BF16)
    for q in range(4):
        out_ref[q, :32] = columns
        out_ref[q, 32:] = rest


def column_index(panel):
    return lax.rem(panel, 8) * 4 + panel // 8


def fetch(source_ref, held_ref, sem):
    copy = pltpu.make_async_copy(source_ref, held_ref, sem)
    copy.start()
    return copy


def times_basis(left_ref, mine_ref, held_ref):
    total = jnp.zeros((left_ref.shape[1], 256), F32)
    for k in range(8):
        for h in (0, 1):
            rows = pl.ds(96 + 256 * h, 256)
            block = jnp.concatenate([mine_ref[k, rows, :], held_ref[k, rows, :]], axis=1)
            total = total + dot(left_ref[2 * k + h], block)
    return total


def in_order(total, ref, *at):
    for half in (0, 1):
        lanes = pl.ds(pl.multiple_of(128 * (lax.axis_index("c") ^ half), 128), 128)
        ref[(*at, lanes)] = total[:, 128 * half : 128 * (half + 1)]


def right_body(col_ref, mine_ref, other_ref, out_ref, held_ref, left_ref, sem):
    copy = fetch(other_ref, held_ref, sem)
    for n in range(16):
        cols = [col_ref[:, 2 * n + s].astype(F32).reshape(96, 128) for s in (0, 1)]
        left_ref[n] = jnp.concatenate(cols, axis=1).astype(BF16)
    copy.wait()
    total = times_basis(left_ref, mine_ref, held_ref).astype(BF16)
    for q in range(4):
        in_order(total, out_ref, q, slice(None))


def left_modes_body(cmaps_ref, pmaps_ref, col_ref, mine_ref, other_ref, out_ref, held_ref, left_ref, sem):
    copy = fetch(other_ref, held_ref, sem)
    first = 2 * lax.axis_index("g")
    for n in range(16):
        pair = []
        for s in (0, 1):
            panel = (2 * n + s) % 4 * 8 + n // 2
            for_leaf = []
            for leaf in range(4):
                row = pmaps_ref[first + leaf // 2, panel]
                for_leaf.append(col_ref[leaf, column_index(cmaps_ref[leaf, row])].astype(F32)[:16])
                for_leaf.append(col_ref[leaf, column_index(row)].astype(F32)[16:])
            pair.append(jnp.concatenate(for_leaf, axis=0))
        left_ref[n] = jnp.concatenate(pair, axis=1).astype(BF16)
    copy.wait()
    in_order(-times_basis(left_ref, mine_ref, held_ref), out_ref, slice(None))


def left_stiff_body(mine_ref, other_ref, half_ref, other_half_ref, after_ref, out_ref, low, high, held_ref, left_ref, sems):
    b = lax.axis_index("b")
    for k, ref in enumerate((half_ref, other_half_ref)):
        for value, rows in enumerate((low, high)):

            @pl.when((b ^ k) == value)
            def _(ref=ref, rows=rows, k=k):
                pltpu.make_async_copy(ref, rows, sems.at[k]).start()

    copy = fetch(other_ref, held_ref, sems.at[2])
    for k in (0, 1):
        pltpu.make_async_copy(half_ref, low, sems.at[k]).wait()
    for n in range(16):
        part = (low, high)[n % 2]
        rows = [part[pl.ds(128 * (8 * s + n // 2), 128), :].astype(F32).T for s in (0, 1)]
        left_ref[n] = jnp.concatenate(rows, axis=1).astype(BF16)
    copy.wait()
    in_order(times_basis(left_ref, mine_ref, held_ref), out_ref, slice(None))


HELD = pltpu.VMEM((8, 608, 128), BF16)


def project(body, out, dtype, specs, scratch, name, *args):
    return pl.pallas_call(
        body,
        out_shape=jax.ShapeDtypeStruct(out, dtype),
        in_specs=specs,
        out_specs=VM,
        scratch_shapes=scratch,
        compiler_params=pltpu.CompilerParams(vmem_limit_bytes=12 << 20),
        cost_estimate=pl.CostEstimate(flops=0, bytes_accessed=0, transcendentals=0),
        name=name,
    )(*args)


def final_body(stiff_ref, modes_ref, right_ref, col_ref, mine_ref, theirs_ref, all_ref):
    left = jnp.concatenate([stiff_ref[...], modes_ref[...]], axis=0).T.astype(BF16)
    for leaf in range(4):
        basis = col_ref[leaf, 32:].astype(F32).reshape(288, 128)
        basis = jnp.concatenate([basis[:128], basis[128:256]], axis=1)
        stacked = jnp.concatenate([basis, right_ref[leaf].astype(F32)], axis=0).astype(BF16)
        all_ref[:, 256 * leaf : 256 * (leaf + 1)] = dot(left, stacked)
    c = lax.axis_index("c")
    mine, theirs = [], []
    for t in range(16):
        mine.append(all_ref[pl.ds(pl.multiple_of(16 * t + 8 * c, 8), 8), :])
        theirs.append(all_ref[pl.ds(pl.multiple_of(16 * t + 8 * (1 - c), 8), 8), :])
    mine_ref[...] = jnp.concatenate(mine, axis=0)
    theirs_ref[...] = jnp.concatenate(theirs, axis=0).astype(BF16)


def swap(value, axis, mask):
    size = lax.axis_size(axis)
    return lax.ppermute(value, axis, [(i, i ^ mask) for i in range(size)])


def exchange(value, axis):
    return lax.all_to_all(value, axis, 0, 0, tiled=True)


def shards(
    child_stiff,
    child_bound,
    child_modes,
    child_inv_eig,
    child_map,
    parent_bound,
    parent_modes,
    parent_inv_eig,
    parent_map,
    interface_basis,
):
    own_basis = interface_basis[0]

    keep, send = regroup(child_stiff[0], child_map, parent_map)
    packed = couple(
        child_modes[0], child_bound[0], child_inv_eig, parent_modes[0], parent_bound[0], parent_inv_eig, own_basis
    )
    near = (keep.astype(F32) + swap(send, "b", 1).astype(F32)).astype(BF16)
    far = swap(near, "a", 1)
    (message,) = call(split_body, [((8, 608, 128), BF16)], [VM], "split", 1_000_000, exchange(packed, "z"))
    mine = exchange(message, ("x", "c"))
    other = swap(mine, "c", 1)
    copies, half = call(
        repeat_body, [((4, 44, 24, 128), BF16), ((2048, 128), BF16)], [VM] * 5, "repeat", 1_000_000,
        mine, own_basis, child_map, near, far,
    )
    other_half = swap(half, "b", 1)
    columns = exchange(copies.reshape(176, 24, 128), LEAF).reshape(4, 44, 24, 128)

    modes_left = pltpu.VMEM((16, 96, 256), BF16)
    one_sem = pltpu.SemaphoreType.DMA(())
    right = project(
        right_body, (4, 96, 256), BF16, [VM, VM, ANY], [HELD, modes_left, one_sem], "right", columns, mine, other
    )
    right = exchange(right.reshape(384, 256), LEAF).reshape(4, 96, 256)
    child_maps = columns[:, 42, 16, :32].astype(jnp.int32)
    modes = project(
        left_modes_body, (96, 256), F32, [SM, SM, VM, VM, ANY], [HELD, modes_left, one_sem], "left_modes",
        child_maps, parent_map, columns, mine, other,
    )
    stiff = project(
        left_stiff_body, (128, 256), F32, [VM, ANY, ANY, ANY, ANY],
        [pltpu.VMEM((2048, 128), BF16)] * 2 + [HELD, pltpu.VMEM((16, 128, 256), BF16), pltpu.SemaphoreType.DMA((3,))],
        "left_stiff", mine, other, half, other_half, modes,
    )
    kept, sent = pl.pallas_call(
        final_body,
        out_shape=[jax.ShapeDtypeStruct((128, 1024), F32), jax.ShapeDtypeStruct((128, 1024), BF16)],
        in_specs=[VM] * 4,
        out_specs=[VM, VM],
        scratch_shapes=[pltpu.VMEM((256, 1024), F32)],
        compiler_params=pltpu.CompilerParams(vmem_limit_bytes=12 << 20),
        cost_estimate=pl.CostEstimate(flops=0, bytes_accessed=0, transcendentals=0),
        name="product",
    )(stiff, modes, right, columns)
    total = (kept + swap(sent, "c", 1).astype(F32)).astype(BF16)
    pieces = exchange(total.reshape(16, 8, 1024), ("z", "x"))
    return jnp.sum(pieces.astype(F32), axis=0)[None]


def solution(mesh):
    names = ("g", "b", "a", "z", "x", "c")
    split = Mesh(mesh.devices.reshape(4, 2, 2, 4, 4, 2), names)
    leaf = ("g", "b", "a")
    placed = (
        P(leaf, None, PANEL),
        P(leaf, PANEL, None),
        P(leaf, None, None),
        P(leaf, None),
        P(leaf, None),
        P(leaf, PANEL, None),
        P(leaf, None, None),
        P(leaf, None),
        P(),
        P(leaf, PANEL, None),
    )
    return jax.shard_map(
        shards, mesh=split, in_specs=placed, out_specs=P(leaf, PANEL, None), check_vma=False
    )
```

```python
import functools

import jax
import jax.numpy as jnp
from jax import lax
from jax.experimental import pallas as pl
from jax.experimental.pallas import tpu as pltpu
from jax.sharding import Mesh
from jax.sharding import PartitionSpec as P

PANEL = ("z", "x", "c")
LEAF = ("b", "a")
F32 = jnp.float32
BF16 = jnp.bfloat16
VM = pl.BlockSpec(memory_space=pltpu.VMEM)
SM = pl.BlockSpec(memory_space=pltpu.SMEM)
ANY = pl.BlockSpec(memory_space=pl.ANY)


def call(body, outs, specs, name, flops, *args):
    shapes = [jax.ShapeDtypeStruct(s, t) for s, t in outs]
    moved = sum(a.size * a.dtype.itemsize for a in args)
    return pl.pallas_call(
        body,
        out_shape=shapes,
        in_specs=specs,
        out_specs=[VM] * len(outs),
        compiler_params=pltpu.CompilerParams(vmem_limit_bytes=12 << 20),
        cost_estimate=pl.CostEstimate(flops=0, bytes_accessed=0, transcendentals=0),
        name=name,
    )(*args)


def dot(left, right):
    return jnp.dot(left, right, preferred_element_type=F32)


def coupling_body(
    cm_ref, cb_ref, ce_ref, pm_ref, pb_ref, pe_ref, u_ref, out_ref, child_ref, parent_ref
):
    step = pl.program_id(0)

    @pl.when(step == 0)
    def _():
        child_ref[...] = jnp.zeros_like(child_ref)
        parent_ref[...] = jnp.zeros_like(parent_ref)

    child_ref[...] += dot(cb_ref[...], cm_ref[...])
    parent_ref[...] += dot(pb_ref[...], pm_ref[...])

    @pl.when(step == pl.num_programs(0) - 1)
    def _():
        child = child_ref[...] * jnp.sqrt(ce_ref[...])
        parent = parent_ref[...] * jnp.sqrt(pe_ref[...])
        both = jnp.concatenate(
            [child.T.reshape(32, 16, 128), parent.T.reshape(32, 8, 128)], axis=1
        ).reshape(768, 128).astype(BF16)
        for z in range(4):
            out_ref[z, :192, :] = both[192 * z : 192 * (z + 1)]
            out_ref[z, 192:320, :] = u_ref[:, :128]
            out_ref[z, 320:, :] = u_ref[:, 128:]


def couple(*args):
    steps = 2
    depth = args[0].shape[0] // steps
    modes = lambda width: pl.BlockSpec((depth, width), lambda i: (i, 0))
    bound = pl.BlockSpec((128, depth), lambda i: (0, i))
    whole = lambda *shape: pl.BlockSpec(shape, lambda i: (0,) * len(shape))
    return pl.pallas_call(
        coupling_body,
        grid=(steps,),
        out_shape=jax.ShapeDtypeStruct((4, 448, 128), BF16),
        in_specs=[modes(512), bound, whole(1, 512), modes(256), bound, whole(1, 256), whole(128, 256)],
        out_specs=whole(4, 448, 128),
        scratch_shapes=[pltpu.VMEM((128, 512), F32), pltpu.VMEM((128, 256), F32)],
        compiler_params=pltpu.CompilerParams(vmem_limit_bytes=60 << 20),
        cost_estimate=pl.CostEstimate(flops=0, bytes_accessed=0, transcendentals=0),
        name="coupling",
    )(*args)


def regroup_body(stiff_ref, cmap_ref, pmap_ref, keep_ref, send_ref, sems):
    b = lax.axis_index("b")
    parent = 2 * lax.axis_index("g") + b
    for i in range(16):
        for k, (ref, half) in enumerate(((keep_ref, b), (send_ref, 1 - b))):
            row = cmap_ref[0, pmap_ref[parent, half * 16 + i]]
            pltpu.make_async_copy(
                stiff_ref.at[pl.ds(pl.multiple_of(row * 128, 128), 128)], ref.at[pl.ds(i * 128, 128)], sems.at[k]
            ).start()
    for k, ref in enumerate((keep_ref, send_ref)):
        pltpu.make_async_copy(stiff_ref.at[pl.ds(0, 2048)], ref, sems.at[k]).wait()


def regroup(*args):
    return pl.pallas_call(
        regroup_body,
        out_shape=[jax.ShapeDtypeStruct((2048, 128), BF16)] * 2,
        in_specs=[ANY, SM, SM],
        out_specs=[VM, VM],
        scratch_shapes=[pltpu.SemaphoreType.DMA((2,))],
        compiler_params=pltpu.CompilerParams(vmem_limit_bytes=12 << 20),
        cost_estimate=pl.CostEstimate(flops=0, bytes_accessed=0, transcendentals=0),
        name="regroup",
    )(*args)


def split_body(got_ref, out_ref):
    parts = [got_ref[z, :192, :].astype(F32).reshape(8, 24, 128) for z in range(4)]
    columns = jnp.concatenate(parts, axis=1).astype(BF16)
    for k in range(8):
        out_ref[k, :96, :] = columns[k]
        for z in range(4):
            at = 192 + 128 * (k % 2)
            out_ref[k, 96 + 128 * z : 224 + 128 * z, :] = got_ref[z, at : at + 128, :]


def repeat_body(one_ref, basis_ref, row_ref, near_ref, far_ref, out_ref, half_ref):
    half_ref[...] = (near_ref[...].astype(F32) + far_ref[...].astype(F32)).astype(BF16)
    row = jnp.concatenate([row_ref[...], jnp.zeros((1, 96), jnp.int32)], axis=1).astype(F32)
    basis = basis_ref[...].astype(F32)
    rest = jnp.concatenate([basis[:, :128], basis[:, 128:], jnp.broadcast_to(row, (32, 128))], axis=0)
    rest = rest.reshape(12, 24, 128).astype(BF16)
    columns = one_ref[:, :96, :].astype(F32).reshape(32, 24, 128).astype(BF16)
    for q in range(4):
        out_ref[q, :32] = columns
        out_ref[q, 32:] = rest


def column_index(panel):
    return lax.rem(panel, 8) * 4 + panel // 8


def times_basis(left_ref, mine_ref, other_ref):
    total = jnp.zeros((left_ref.shape[1], 256), F32)
    for k in range(8):
        for h in (0, 1):
            rows = pl.ds(96 + 256 * h, 256)
            block = jnp.concatenate([mine_ref[k, rows, :], other_ref[k, rows, :]], axis=1)
            total = total + dot(left_ref[2 * k + h], block)
    return total


def in_order(total, ref, *at):
    for half in (0, 1):
        lanes = pl.ds(pl.multiple_of(128 * (lax.axis_index("c") ^ half), 128), 128)
        ref[(*at, lanes)] = total[:, 128 * half : 128 * (half + 1)]


def right_body(col_ref, mine_ref, other_ref, out_ref, left_ref):
    for n in range(16):
        cols = [col_ref[:, 2 * n + s].astype(F32).reshape(96, 128) for s in (0, 1)]
        left_ref[n] = jnp.concatenate(cols, axis=1).astype(BF16)
    total = times_basis(left_ref, mine_ref, other_ref).astype(BF16)
    for q in range(4):
        in_order(total, out_ref, q, slice(None))


def left_modes_body(cmaps_ref, pmaps_ref, col_ref, mine_ref, other_ref, out_ref, left_ref):
    first = 2 * lax.axis_index("g")
    for n in range(16):
        pair = []
        for s in (0, 1):
            panel = (2 * n + s) % 4 * 8 + n // 2
            for_leaf = []
            for leaf in range(4):
                row = pmaps_ref[first + leaf // 2, panel]
                for_leaf.append(col_ref[leaf, column_index(cmaps_ref[leaf, row])].astype(F32)[:16])
                for_leaf.append(col_ref[leaf, column_index(row)].astype(F32)[16:])
            pair.append(jnp.concatenate(for_leaf, axis=0))
        left_ref[n] = jnp.concatenate(pair, axis=1).astype(BF16)
    in_order(-times_basis(left_ref, mine_ref, other_ref), out_ref, slice(None))


def left_stiff_body(mine_ref, other_ref, half_ref, other_half_ref, after_ref, out_ref, low, high, left_ref, sems):
    b = lax.axis_index("b")
    for k, ref in enumerate((half_ref, other_half_ref)):
        for value, rows in enumerate((low, high)):

            @pl.when((b ^ k) == value)
            def _(ref=ref, rows=rows, k=k):
                pltpu.make_async_copy(ref, rows, sems.at[k]).start()

    for k in (0, 1):
        pltpu.make_async_copy(half_ref, low, sems.at[k]).wait()
    for n in range(16):
        part = (low, high)[n % 2]
        rows = [part[pl.ds(128 * (8 * s + n // 2), 128), :].astype(F32).T for s in (0, 1)]
        left_ref[n] = jnp.concatenate(rows, axis=1).astype(BF16)
    in_order(times_basis(left_ref, mine_ref, other_ref), out_ref, slice(None))


def project(body, out, dtype, specs, scratch, name, *args):
    return pl.pallas_call(
        body,
        out_shape=jax.ShapeDtypeStruct(out, dtype),
        in_specs=specs,
        out_specs=VM,
        scratch_shapes=scratch,
        compiler_params=pltpu.CompilerParams(vmem_limit_bytes=12 << 20),
        cost_estimate=pl.CostEstimate(flops=0, bytes_accessed=0, transcendentals=0),
        name=name,
    )(*args)


def final_body(stiff_ref, modes_ref, right_ref, col_ref, mine_ref, theirs_ref, all_ref):
    left = jnp.concatenate([stiff_ref[...], modes_ref[...]], axis=0).T.astype(BF16)
    for leaf in range(4):
        basis = col_ref[leaf, 32:].astype(F32).reshape(288, 128)
        basis = jnp.concatenate([basis[:128], basis[128:256]], axis=1)
        stacked = jnp.concatenate([basis, right_ref[leaf].astype(F32)], axis=0).astype(BF16)
        all_ref[:, 256 * leaf : 256 * (leaf + 1)] = dot(left, stacked)
    c = lax.axis_index("c")
    mine, theirs = [], []
    for t in range(16):
        mine.append(all_ref[pl.ds(pl.multiple_of(16 * t + 8 * c, 8), 8), :])
        theirs.append(all_ref[pl.ds(pl.multiple_of(16 * t + 8 * (1 - c), 8), 8), :])
    mine_ref[...] = jnp.concatenate(mine, axis=0)
    theirs_ref[...] = jnp.concatenate(theirs, axis=0).astype(BF16)


def swap(value, axis, mask):
    size = lax.axis_size(axis)
    return lax.ppermute(value, axis, [(i, i ^ mask) for i in range(size)])


def exchange(value, axis):
    return lax.all_to_all(value, axis, 0, 0, tiled=True)


def shards(
    child_stiff,
    child_bound,
    child_modes,
    child_inv_eig,
    child_map,
    parent_bound,
    parent_modes,
    parent_inv_eig,
    parent_map,
    interface_basis,
):
    own_basis = interface_basis[0]

    keep, send = regroup(child_stiff[0], child_map, parent_map)
    packed = couple(
        child_modes[0], child_bound[0], child_inv_eig, parent_modes[0], parent_bound[0], parent_inv_eig, own_basis
    )
    near = (keep.astype(F32) + swap(send, "b", 1).astype(F32)).astype(BF16)
    far = swap(near, "a", 1)
    (message,) = call(split_body, [((8, 608, 128), BF16)], [VM], "split", 1_000_000, exchange(packed, "z"))
    mine = exchange(message, ("x", "c"))
    other = swap(mine, "c", 1)
    copies, half = call(
        repeat_body, [((4, 44, 24, 128), BF16), ((2048, 128), BF16)], [VM] * 5, "repeat", 1_000_000,
        mine, own_basis, child_map, near, far,
    )
    other_half = swap(half, "b", 1)
    columns = exchange(copies.reshape(176, 24, 128), LEAF).reshape(4, 44, 24, 128)

    modes_left = pltpu.VMEM((16, 96, 256), BF16)
    right = project(
        right_body, (4, 96, 256), BF16, [VM, VM, VM], [modes_left], "right", columns, mine, other
    )
    right = exchange(right.reshape(384, 256), LEAF).reshape(4, 96, 256)
    child_maps = columns[:, 42, 16, :32].astype(jnp.int32)
    modes = project(
        left_modes_body, (96, 256), F32, [SM, SM, VM, VM, VM], [modes_left], "left_modes",
        child_maps, parent_map, columns, mine, other,
    )
    stiff = project(
        left_stiff_body, (128, 256), F32, [VM, VM, ANY, ANY, ANY],
        [pltpu.VMEM((2048, 128), BF16)] * 2 + [pltpu.VMEM((16, 128, 256), BF16), pltpu.SemaphoreType.DMA((2,))],
        "left_stiff", mine, other, half, other_half, modes,
    )
    kept, sent = pl.pallas_call(
        final_body,
        out_shape=[jax.ShapeDtypeStruct((128, 1024), F32), jax.ShapeDtypeStruct((128, 1024), BF16)],
        in_specs=[VM] * 4,
        out_specs=[VM, VM],
        scratch_shapes=[pltpu.VMEM((256, 1024), F32)],
        compiler_params=pltpu.CompilerParams(vmem_limit_bytes=12 << 20),
        cost_estimate=pl.CostEstimate(flops=0, bytes_accessed=0, transcendentals=0),
        name="product",
    )(stiff, modes, right, columns)
    total = (kept + swap(sent, "c", 1).astype(F32)).astype(BF16)
    pieces = exchange(total.reshape(16, 8, 1024), ("z", "x"))
    return jnp.sum(pieces.astype(F32), axis=0)[None]


def solution(mesh):
    names = ("g", "b", "a", "z", "x", "c")
    split = Mesh(mesh.devices.reshape(4, 2, 2, 4, 4, 2), names)
    leaf = ("g", "b", "a")
    placed = (
        P(leaf, None, PANEL),
        P(leaf, PANEL, None),
        P(leaf, None, None),
        P(leaf, None),
        P(leaf, None),
        P(leaf, PANEL, None),
        P(leaf, None, None),
        P(leaf, None),
        P(),
        P(leaf, PANEL, None),
    )
    return jax.shard_map(
        shards, mesh=split, in_specs=placed, out_specs=P(leaf, PANEL, None), check_vma=False
    )
```

```python
import functools

import jax
import jax.numpy as jnp
from jax import lax
from jax.experimental import pallas as pl
from jax.experimental.pallas import tpu as pltpu
from jax.sharding import Mesh
from jax.sharding import PartitionSpec as P

PANEL = ("z", "x", "c")
LEAF = ("b", "a")
F32 = jnp.float32
BF16 = jnp.bfloat16
VM = pl.BlockSpec(memory_space=pltpu.VMEM)
SM = pl.BlockSpec(memory_space=pltpu.SMEM)
ANY = pl.BlockSpec(memory_space=pl.ANY)


def call(body, outs, specs, name, flops, *args):
    shapes = [jax.ShapeDtypeStruct(s, t) for s, t in outs]
    moved = sum(a.size * a.dtype.itemsize for a in args)
    return pl.pallas_call(
        body,
        out_shape=shapes,
        in_specs=specs,
        out_specs=[VM] * len(outs),
        compiler_params=pltpu.CompilerParams(vmem_limit_bytes=12 << 20),
        cost_estimate=pl.CostEstimate(flops=0, bytes_accessed=0, transcendentals=0),
        name=name,
    )(*args)


def dot(left, right):
    return jnp.dot(left, right, preferred_element_type=F32)


def coupling_body(
    cm_ref, cb_ref, ce_ref, pm_ref, pb_ref, pe_ref, u_ref, out_ref, child_ref, parent_ref
):
    step = pl.program_id(0)

    @pl.when(step == 0)
    def _():
        child_ref[...] = jnp.zeros_like(child_ref)
        parent_ref[...] = jnp.zeros_like(parent_ref)

    child_ref[...] += dot(cb_ref[...], cm_ref[...])
    parent_ref[...] += dot(pb_ref[...], pm_ref[...])

    @pl.when(step == pl.num_programs(0) - 1)
    def _():
        child = child_ref[...] * jnp.sqrt(ce_ref[...])
        parent = parent_ref[...] * jnp.sqrt(pe_ref[...])
        both = jnp.concatenate(
            [child.T.reshape(32, 16, 128), parent.T.reshape(32, 8, 128)], axis=1
        ).reshape(768, 128).astype(BF16)
        for z in range(4):
            out_ref[z, :192, :] = both[192 * z : 192 * (z + 1)]
            out_ref[z, 192:320, :] = u_ref[:, :128]
            out_ref[z, 320:, :] = u_ref[:, 128:]


def couple(*args):
    steps = 2
    depth = args[0].shape[0] // steps
    modes = lambda width: pl.BlockSpec((depth, width), lambda i: (i, 0))
    bound = pl.BlockSpec((128, depth), lambda i: (0, i))
    whole = lambda *shape: pl.BlockSpec(shape, lambda i: (0,) * len(shape))
    return pl.pallas_call(
        coupling_body,
        grid=(steps,),
        out_shape=jax.ShapeDtypeStruct((4, 448, 128), BF16),
        in_specs=[modes(512), bound, whole(1, 512), modes(256), bound, whole(1, 256), whole(128, 256)],
        out_specs=whole(4, 448, 128),
        scratch_shapes=[pltpu.VMEM((128, 512), F32), pltpu.VMEM((128, 256), F32)],
        compiler_params=pltpu.CompilerParams(vmem_limit_bytes=60 << 20),
        cost_estimate=pl.CostEstimate(flops=0, bytes_accessed=0, transcendentals=0),
        name="coupling",
    )(*args)


def regroup_body(stiff_ref, cmap_ref, pmap_ref, keep_ref, send_ref, sems):
    b = lax.axis_index("b")
    parent = 2 * lax.axis_index("g") + b
    for i in range(16):
        for k, (ref, half) in enumerate(((keep_ref, b), (send_ref, 1 - b))):
            row = cmap_ref[0, pmap_ref[parent, half * 16 + i]]
            pltpu.make_async_copy(
                stiff_ref.at[pl.ds(pl.multiple_of(row * 128, 128), 128)], ref.at[pl.ds(i * 128, 128)], sems.at[k]
            ).start()
    for k, ref in enumerate((keep_ref, send_ref)):
        pltpu.make_async_copy(stiff_ref.at[pl.ds(0, 2048)], ref, sems.at[k]).wait()


def regroup(*args):
    return pl.pallas_call(
        regroup_body,
        out_shape=[jax.ShapeDtypeStruct((2048, 128), BF16)] * 2,
        in_specs=[ANY, SM, SM],
        out_specs=[VM, VM],
        scratch_shapes=[pltpu.SemaphoreType.DMA((2,))],
        compiler_params=pltpu.CompilerParams(vmem_limit_bytes=12 << 20),
        cost_estimate=pl.CostEstimate(flops=0, bytes_accessed=0, transcendentals=0),
        name="regroup",
    )(*args)


def split_body(got_ref, out_ref):
    parts = [got_ref[z, :192, :].astype(F32).reshape(8, 24, 128) for z in range(4)]
    columns = jnp.concatenate(parts, axis=1).astype(BF16)
    for k in range(8):
        out_ref[k, :96, :] = columns[k]
        for z in range(4):
            at = 192 + 128 * (k % 2)
            out_ref[k, 96 + 128 * z : 224 + 128 * z, :] = got_ref[z, at : at + 128, :]


def repeat_body(one_ref, basis_ref, row_ref, near_ref, far_ref, out_ref, half_ref):
    half_ref[...] = (near_ref[...].astype(F32) + far_ref[...].astype(F32)).astype(BF16)
    row = jnp.concatenate([row_ref[...], jnp.zeros((1, 96), jnp.int32)], axis=1).astype(F32)
    basis = basis_ref[...].astype(F32)
    rest = jnp.concatenate([basis[:, :128], basis[:, 128:], jnp.broadcast_to(row, (32, 128))], axis=0)
    rest = rest.reshape(12, 24, 128).astype(BF16)
    columns = one_ref[:, :96, :].astype(F32).reshape(32, 24, 128).astype(BF16)
    for q in range(4):
        out_ref[q, :32] = columns
        out_ref[q, 32:] = rest


def column_index(panel):
    return lax.rem(panel, 8) * 4 + panel // 8


def times_basis(left_ref, mine_ref, other_ref):
    total = jnp.zeros((left_ref.shape[1], 256), F32)
    for k in range(8):
        for h in (0, 1):
            rows = pl.ds(96 + 256 * h, 256)
            block = jnp.concatenate([mine_ref[k, rows, :], other_ref[k, rows, :]], axis=1)
            total = total + dot(left_ref[2 * k + h], block)
    return total


def in_order(total, ref, *at):
    for half in (0, 1):
        lanes = pl.ds(pl.multiple_of(128 * (lax.axis_index("c") ^ half), 128), 128)
        ref[(*at, lanes)] = total[:, 128 * half : 128 * (half + 1)]


def right_half(col_ref, basis_ref):
    total = jnp.zeros((96, 128), F32)
    for n in range(16):
        cols = [col_ref[:, 2 * n + s].astype(F32).reshape(96, 128) for s in (0, 1)]
        block = basis_ref[n // 2, pl.ds(96 + 256 * (n % 2), 256), :]
        total = total + dot(jnp.concatenate(cols, axis=1).astype(BF16), block)
    return total


def right_mine_body(col_ref, mine_ref, out_ref):
    out_ref[...] = right_half(col_ref, mine_ref)


def right_other_body(col_ref, other_ref, part_ref, out_ref):
    total = jnp.concatenate([part_ref[...], right_half(col_ref, other_ref)], axis=1).astype(BF16)
    for q in range(4):
        in_order(total, out_ref, q, slice(None))


def left_modes_body(cmaps_ref, pmaps_ref, col_ref, mine_ref, other_ref, half_ref, out_ref, near_ref, left_ref):
    near_ref[...] = stiff_part(half_ref, lax.axis_index("b"), mine_ref, other_ref)
    first = 2 * lax.axis_index("g")
    for n in range(16):
        pair = []
        for s in (0, 1):
            panel = (2 * n + s) % 4 * 8 + n // 2
            for_leaf = []
            for leaf in range(4):
                row = pmaps_ref[first + leaf // 2, panel]
                for_leaf.append(col_ref[leaf, column_index(cmaps_ref[leaf, row])].astype(F32)[:16])
                for_leaf.append(col_ref[leaf, column_index(row)].astype(F32)[16:])
            pair.append(jnp.concatenate(for_leaf, axis=0))
        left_ref[n] = jnp.concatenate(pair, axis=1).astype(BF16)
    in_order(-times_basis(left_ref, mine_ref, other_ref), out_ref, slice(None))


def stiff_part(rows_ref, side, mine_ref, other_ref):
    total = jnp.zeros((128, 256), F32)
    for k in range(8):
        rows = [rows_ref[pl.ds(128 * (8 * s + k), 128), :].astype(F32).T for s in (0, 1)]
        at = pl.ds(pl.multiple_of(96 + 256 * side, 32), 256)
        block = jnp.concatenate([mine_ref[k, at, :], other_ref[k, at, :]], axis=1)
        total = total + dot(jnp.concatenate(rows, axis=1).astype(BF16), block)
    return total


def left_stiff_body(mine_ref, other_ref, other_half_ref, near_ref, out_ref):
    total = near_ref[...] + stiff_part(other_half_ref, 1 - lax.axis_index("b"), mine_ref, other_ref)
    in_order(total, out_ref, slice(None))


def project(body, out, dtype, specs, scratch, name, *args):
    return pl.pallas_call(
        body,
        out_shape=jax.ShapeDtypeStruct(out, dtype),
        in_specs=specs,
        out_specs=VM,
        scratch_shapes=scratch,
        compiler_params=pltpu.CompilerParams(vmem_limit_bytes=12 << 20),
        cost_estimate=pl.CostEstimate(flops=0, bytes_accessed=0, transcendentals=0),
        name=name,
    )(*args)


def final_body(stiff_ref, modes_ref, right_ref, col_ref, mine_ref, theirs_ref, all_ref):
    left = jnp.concatenate([stiff_ref[...], modes_ref[...]], axis=0).T.astype(BF16)
    for leaf in range(4):
        basis = col_ref[leaf, 32:].astype(F32).reshape(288, 128)
        basis = jnp.concatenate([basis[:128], basis[128:256]], axis=1)
        stacked = jnp.concatenate([basis, right_ref[leaf].astype(F32)], axis=0).astype(BF16)
        all_ref[:, 256 * leaf : 256 * (leaf + 1)] = dot(left, stacked)
    c = lax.axis_index("c")
    mine, theirs = [], []
    for t in range(16):
        mine.append(all_ref[pl.ds(pl.multiple_of(16 * t + 8 * c, 8), 8), :])
        theirs.append(all_ref[pl.ds(pl.multiple_of(16 * t + 8 * (1 - c), 8), 8), :])
    mine_ref[...] = jnp.concatenate(mine, axis=0)
    theirs_ref[...] = jnp.concatenate(theirs, axis=0).astype(BF16)


def swap(value, axis, mask):
    size = lax.axis_size(axis)
    return lax.ppermute(value, axis, [(i, i ^ mask) for i in range(size)])


def exchange(value, axis):
    return lax.all_to_all(value, axis, 0, 0, tiled=True)


def shards(
    child_stiff,
    child_bound,
    child_modes,
    child_inv_eig,
    child_map,
    parent_bound,
    parent_modes,
    parent_inv_eig,
    parent_map,
    interface_basis,
):
    own_basis = interface_basis[0]

    keep, send = regroup(child_stiff[0], child_map, parent_map)
    packed = couple(
        child_modes[0], child_bound[0], child_inv_eig, parent_modes[0], parent_bound[0], parent_inv_eig, own_basis
    )
    near = (keep.astype(F32) + swap(send, "b", 1).astype(F32)).astype(BF16)
    far = swap(near, "a", 1)
    (message,) = call(split_body, [((8, 608, 128), BF16)], [VM], "split", 1_000_000, exchange(packed, "z"))
    mine = exchange(message, ("x", "c"))
    other = swap(mine, "c", 1)
    copies, half = call(
        repeat_body, [((4, 44, 24, 128), BF16), ((2048, 128), BF16)], [VM] * 5, "repeat", 1_000_000,
        mine, own_basis, child_map, near, far,
    )
    other_half = swap(half, "b", 1)
    columns = exchange(copies.reshape(176, 24, 128), LEAF).reshape(4, 44, 24, 128)

    modes_left = pltpu.VMEM((16, 96, 256), BF16)
    part = project(right_mine_body, (96, 128), F32, [VM, VM], [], "right_mine", columns, mine)
    right = project(right_other_body, (4, 96, 256), BF16, [VM] * 3, [], "right_other", columns, other, part)
    right = exchange(right.reshape(384, 256), LEAF).reshape(4, 96, 256)
    child_maps = columns[:, 42, 16, :32].astype(jnp.int32)
    modes, near_stiff = pl.pallas_call(
        left_modes_body,
        out_shape=[jax.ShapeDtypeStruct((96, 256), F32), jax.ShapeDtypeStruct((128, 256), F32)],
        in_specs=[SM, SM] + [VM] * 4,
        out_specs=[VM, VM],
        scratch_shapes=[modes_left],
        compiler_params=pltpu.CompilerParams(vmem_limit_bytes=12 << 20),
        cost_estimate=pl.CostEstimate(flops=0, bytes_accessed=0, transcendentals=0),
        name="left_modes",
    )(child_maps, parent_map, columns, mine, other, half)
    stiff = project(
        left_stiff_body, (128, 256), F32, [VM] * 4, [], "left_stiff", mine, other, other_half, near_stiff
    )
    kept, sent = pl.pallas_call(
        final_body,
        out_shape=[jax.ShapeDtypeStruct((128, 1024), F32), jax.ShapeDtypeStruct((128, 1024), BF16)],
        in_specs=[VM] * 4,
        out_specs=[VM, VM],
        scratch_shapes=[pltpu.VMEM((256, 1024), F32)],
        compiler_params=pltpu.CompilerParams(vmem_limit_bytes=12 << 20),
        cost_estimate=pl.CostEstimate(flops=0, bytes_accessed=0, transcendentals=0),
        name="product",
    )(stiff, modes, right, columns)
    total = (kept + swap(sent, "c", 1).astype(F32)).astype(BF16)
    pieces = exchange(total.reshape(16, 8, 1024), ("z", "x"))
    return jnp.sum(pieces.astype(F32), axis=0)[None]


def solution(mesh):
    names = ("g", "b", "a", "z", "x", "c")
    split = Mesh(mesh.devices.reshape(4, 2, 2, 4, 4, 2), names)
    leaf = ("g", "b", "a")
    placed = (
        P(leaf, None, PANEL),
        P(leaf, PANEL, None),
        P(leaf, None, None),
        P(leaf, None),
        P(leaf, None),
        P(leaf, PANEL, None),
        P(leaf, None, None),
        P(leaf, None),
        P(),
        P(leaf, PANEL, None),
    )
    return jax.shard_map(
        shards, mesh=split, in_specs=placed, out_specs=P(leaf, PANEL, None), check_vma=False
    )
```

```python
import functools

import jax
import jax.numpy as jnp
from jax import lax
from jax.experimental import pallas as pl
from jax.experimental.pallas import tpu as pltpu
from jax.sharding import Mesh
from jax.sharding import PartitionSpec as P

PANEL = ("z", "x", "c")
LEAF = ("b", "a")
F32 = jnp.float32
BF16 = jnp.bfloat16
VM = pl.BlockSpec(memory_space=pltpu.VMEM)
SM = pl.BlockSpec(memory_space=pltpu.SMEM)
ANY = pl.BlockSpec(memory_space=pl.ANY)


def call(body, outs, specs, name, flops, *args):
    shapes = [jax.ShapeDtypeStruct(s, t) for s, t in outs]
    moved = sum(a.size * a.dtype.itemsize for a in args)
    return pl.pallas_call(
        body,
        out_shape=shapes,
        in_specs=specs,
        out_specs=[VM] * len(outs),
        compiler_params=pltpu.CompilerParams(vmem_limit_bytes=12 << 20),
        cost_estimate=pl.CostEstimate(flops=0, bytes_accessed=0, transcendentals=0),
        name=name,
    )(*args)


def dot(left, right):
    return jnp.dot(left, right, preferred_element_type=F32)


def coupling_body(
    cm_ref, cb_ref, ce_ref, pm_ref, pb_ref, pe_ref, u_ref, out_ref, child_ref, parent_ref
):
    step = pl.program_id(0)

    @pl.when(step == 0)
    def _():
        child_ref[...] = jnp.zeros_like(child_ref)
        parent_ref[...] = jnp.zeros_like(parent_ref)

    child_ref[...] += dot(cb_ref[...], cm_ref[...])
    parent_ref[...] += dot(pb_ref[...], pm_ref[...])

    @pl.when(step == pl.num_programs(0) - 1)
    def _():
        child = child_ref[...] * jnp.sqrt(ce_ref[...])
        parent = parent_ref[...] * jnp.sqrt(pe_ref[...])
        both = jnp.concatenate(
            [child.T.reshape(32, 16, 128), parent.T.reshape(32, 8, 128)], axis=1
        ).reshape(768, 128).astype(BF16)
        for z in range(4):
            out_ref[z, :192, :] = both[192 * z : 192 * (z + 1)]
            out_ref[z, 192:320, :] = u_ref[:, :128]
            out_ref[z, 320:, :] = u_ref[:, 128:]


def couple(*args):
    steps = 2
    depth = args[0].shape[0] // steps
    modes = lambda width: pl.BlockSpec((depth, width), lambda i: (i, 0))
    bound = pl.BlockSpec((128, depth), lambda i: (0, i))
    whole = lambda *shape: pl.BlockSpec(shape, lambda i: (0,) * len(shape))
    return pl.pallas_call(
        coupling_body,
        grid=(steps,),
        out_shape=jax.ShapeDtypeStruct((4, 448, 128), BF16),
        in_specs=[modes(512), bound, whole(1, 512), modes(256), bound, whole(1, 256), whole(128, 256)],
        out_specs=whole(4, 448, 128),
        scratch_shapes=[pltpu.VMEM((128, 512), F32), pltpu.VMEM((128, 256), F32)],
        compiler_params=pltpu.CompilerParams(vmem_limit_bytes=60 << 20),
        cost_estimate=pl.CostEstimate(flops=0, bytes_accessed=0, transcendentals=0),
        name="coupling",
    )(*args)


def regroup_body(stiff_ref, cmap_ref, pmap_ref, keep_ref, send_ref, sems):
    b = lax.axis_index("b")
    parent = 2 * lax.axis_index("g") + b
    for i in range(16):
        for k, (ref, half) in enumerate(((keep_ref, b), (send_ref, 1 - b))):
            row = cmap_ref[0, pmap_ref[parent, half * 16 + i]]
            pltpu.make_async_copy(
                stiff_ref.at[pl.ds(pl.multiple_of(row * 128, 128), 128)], ref.at[pl.ds(i * 128, 128)], sems.at[k]
            ).start()
    for k, ref in enumerate((keep_ref, send_ref)):
        pltpu.make_async_copy(stiff_ref.at[pl.ds(0, 2048)], ref, sems.at[k]).wait()


def regroup(*args):
    return pl.pallas_call(
        regroup_body,
        out_shape=[jax.ShapeDtypeStruct((2048, 128), BF16)] * 2,
        in_specs=[ANY, SM, SM],
        out_specs=[VM, VM],
        scratch_shapes=[pltpu.SemaphoreType.DMA((2,))],
        compiler_params=pltpu.CompilerParams(vmem_limit_bytes=12 << 20),
        cost_estimate=pl.CostEstimate(flops=0, bytes_accessed=0, transcendentals=0),
        name="regroup",
    )(*args)


def split_body(got_ref, out_ref):
    parts = [got_ref[z, :192, :].astype(F32).reshape(8, 24, 128) for z in range(4)]
    columns = jnp.concatenate(parts, axis=1).astype(BF16)
    for k in range(8):
        out_ref[k, :96, :] = columns[k]
        for z in range(4):
            at = 192 + 128 * (k % 2)
            out_ref[k, 96 + 128 * z : 224 + 128 * z, :] = got_ref[z, at : at + 128, :]


def repeat_body(one_ref, basis_ref, row_ref, near_ref, far_ref, out_ref, half_ref):
    half_ref[...] = (near_ref[...].astype(F32) + far_ref[...].astype(F32)).astype(BF16)
    row = jnp.concatenate([row_ref[...], jnp.zeros((1, 96), jnp.int32)], axis=1).astype(F32)
    basis = basis_ref[...].astype(F32)
    rest = jnp.concatenate([basis[:, :128], basis[:, 128:], jnp.broadcast_to(row, (32, 128))], axis=0)
    rest = rest.reshape(12, 24, 128).astype(BF16)
    columns = one_ref[:, :96, :].astype(F32).reshape(32, 24, 128).astype(BF16)
    for q in range(4):
        out_ref[q, :32] = columns
        out_ref[q, 32:] = rest


def column_index(panel):
    return lax.rem(panel, 8) * 4 + panel // 8


def times_basis(left_ref, mine_ref, other_ref):
    total = jnp.zeros((left_ref.shape[1], 256), F32)
    for k in range(8):
        for h in (0, 1):
            rows = pl.ds(96 + 256 * h, 256)
            block = jnp.concatenate([mine_ref[k, rows, :], other_ref[k, rows, :]], axis=1)
            total = total + dot(left_ref[2 * k + h], block)
    return total


def in_order(total, ref, *at):
    for half in (0, 1):
        lanes = pl.ds(pl.multiple_of(128 * (lax.axis_index("c") ^ half), 128), 128)
        ref[(*at, lanes)] = total[:, 128 * half : 128 * (half + 1)]


def right_half(col_ref, basis_ref):
    total = jnp.zeros((96, 128), F32)
    for n in range(16):
        cols = [col_ref[:, 2 * n + s].astype(F32).reshape(96, 128) for s in (0, 1)]
        block = basis_ref[n // 2, pl.ds(96 + 256 * (n % 2), 256), :]
        total = total + dot(jnp.concatenate(cols, axis=1).astype(BF16), block)
    return total


def right_mine_body(col_ref, mine_ref, out_ref):
    out_ref[...] = right_half(col_ref, mine_ref)


def right_other_body(col_ref, other_ref, part_ref, out_ref):
    total = jnp.concatenate([part_ref[...], right_half(col_ref, other_ref)], axis=1).astype(BF16)
    for q in range(4):
        in_order(total, out_ref, q, slice(None))


def left_modes_body(cmaps_ref, pmaps_ref, col_ref, mine_ref, other_ref, half_ref, out_ref, near_ref, left_ref):
    near_ref[...] = stiff_part(half_ref, lax.axis_index("b"), mine_ref, other_ref)
    first = 2 * lax.axis_index("g")
    for n in range(16):
        pair = []
        for s in (0, 1):
            panel = (2 * n + s) % 4 * 8 + n // 2
            for_leaf = []
            for leaf in range(4):
                row = pmaps_ref[first + leaf // 2, panel]
                for_leaf.append(col_ref[leaf, column_index(cmaps_ref[leaf, row])].astype(F32)[:16])
                for_leaf.append(col_ref[leaf, column_index(row)].astype(F32)[16:])
            pair.append(jnp.concatenate(for_leaf, axis=0))
        left_ref[n] = jnp.concatenate(pair, axis=1).astype(BF16)
    in_order(-times_basis(left_ref, mine_ref, other_ref), out_ref, slice(None))


def stiff_part(rows_ref, side, mine_ref, other_ref):
    total = jnp.zeros((128, 256), F32)
    for k in range(8):
        rows = [rows_ref[pl.ds(128 * (8 * s + k), 128), :].astype(F32).T for s in (0, 1)]
        at = pl.ds(pl.multiple_of(96 + 256 * side, 32), 256)
        block = jnp.concatenate([mine_ref[k, at, :], other_ref[k, at, :]], axis=1)
        total = total + dot(jnp.concatenate(rows, axis=1).astype(BF16), block)
    return total


def left_stiff_body(mine_ref, other_ref, other_half_ref, near_ref, out_ref, rows_ref, held_ref, sems):
    at = pl.ds(pl.multiple_of(96 + 256 * (1 - lax.axis_index("b")), 32), 256)
    copies = [
        pltpu.make_async_copy(other_half_ref, rows_ref, sems.at[0]),
        pltpu.make_async_copy(other_ref.at[:, at, :], held_ref, sems.at[1]),
    ]
    for copy in copies:
        copy.start()
    for copy in copies:
        copy.wait()
    total = near_ref[...]
    for k in range(8):
        rows = [rows_ref[pl.ds(128 * (8 * s + k), 128), :].astype(F32).T for s in (0, 1)]
        block = jnp.concatenate([mine_ref[k, at, :], held_ref[k]], axis=1)
        total = total + dot(jnp.concatenate(rows, axis=1).astype(BF16), block)
    in_order(total, out_ref, slice(None))


def project(body, out, dtype, specs, scratch, name, *args):
    return pl.pallas_call(
        body,
        out_shape=jax.ShapeDtypeStruct(out, dtype),
        in_specs=specs,
        out_specs=VM,
        scratch_shapes=scratch,
        compiler_params=pltpu.CompilerParams(vmem_limit_bytes=12 << 20),
        cost_estimate=pl.CostEstimate(flops=0, bytes_accessed=0, transcendentals=0),
        name=name,
    )(*args)


def final_body(stiff_ref, modes_ref, right_ref, col_ref, mine_ref, theirs_ref, all_ref):
    left = jnp.concatenate([stiff_ref[...], modes_ref[...]], axis=0).T.astype(BF16)
    for leaf in range(4):
        basis = col_ref[leaf, 32:].astype(F32).reshape(288, 128)
        basis = jnp.concatenate([basis[:128], basis[128:256]], axis=1)
        stacked = jnp.concatenate([basis, right_ref[leaf].astype(F32)], axis=0).astype(BF16)
        all_ref[:, 256 * leaf : 256 * (leaf + 1)] = dot(left, stacked)
    c = lax.axis_index("c")
    mine, theirs = [], []
    for t in range(16):
        mine.append(all_ref[pl.ds(pl.multiple_of(16 * t + 8 * c, 8), 8), :])
        theirs.append(all_ref[pl.ds(pl.multiple_of(16 * t + 8 * (1 - c), 8), 8), :])
    mine_ref[...] = jnp.concatenate(mine, axis=0)
    theirs_ref[...] = jnp.concatenate(theirs, axis=0).astype(BF16)


def swap(value, axis, mask):
    size = lax.axis_size(axis)
    return lax.ppermute(value, axis, [(i, i ^ mask) for i in range(size)])


def exchange(value, axis):
    return lax.all_to_all(value, axis, 0, 0, tiled=True)


def shards(
    child_stiff,
    child_bound,
    child_modes,
    child_inv_eig,
    child_map,
    parent_bound,
    parent_modes,
    parent_inv_eig,
    parent_map,
    interface_basis,
):
    own_basis = interface_basis[0]

    keep, send = regroup(child_stiff[0], child_map, parent_map)
    packed = couple(
        child_modes[0], child_bound[0], child_inv_eig, parent_modes[0], parent_bound[0], parent_inv_eig, own_basis
    )
    near = (keep.astype(F32) + swap(send, "b", 1).astype(F32)).astype(BF16)
    far = swap(near, "a", 1)
    (message,) = call(split_body, [((8, 608, 128), BF16)], [VM], "split", 1_000_000, exchange(packed, "z"))
    mine = exchange(message, ("x", "c"))
    other = swap(mine, "c", 1)
    copies, half = call(
        repeat_body, [((4, 44, 24, 128), BF16), ((2048, 128), BF16)], [VM] * 5, "repeat", 1_000_000,
        mine, own_basis, child_map, near, far,
    )
    other_half = swap(half, "b", 1)
    columns = exchange(copies.reshape(176, 24, 128), LEAF).reshape(4, 44, 24, 128)

    modes_left = pltpu.VMEM((16, 96, 256), BF16)
    part = project(right_mine_body, (96, 128), F32, [VM, VM], [], "right_mine", columns, mine)
    right = project(right_other_body, (4, 96, 256), BF16, [VM] * 3, [], "right_other", columns, other, part)
    right = exchange(right.reshape(384, 256), LEAF).reshape(4, 96, 256)
    child_maps = columns[:, 42, 16, :32].astype(jnp.int32)
    modes, near_stiff = pl.pallas_call(
        left_modes_body,
        out_shape=[jax.ShapeDtypeStruct((96, 256), F32), jax.ShapeDtypeStruct((128, 256), F32)],
        in_specs=[SM, SM] + [VM] * 4,
        out_specs=[VM, VM],
        scratch_shapes=[modes_left],
        compiler_params=pltpu.CompilerParams(vmem_limit_bytes=12 << 20),
        cost_estimate=pl.CostEstimate(flops=0, bytes_accessed=0, transcendentals=0),
        name="left_modes",
    )(child_maps, parent_map, columns, mine, other, half)
    stiff = project(
        left_stiff_body, (128, 256), F32, [VM, ANY, ANY, VM],
        [pltpu.VMEM((2048, 128), BF16), pltpu.VMEM((8, 256, 128), BF16), pltpu.SemaphoreType.DMA((2,))],
        "left_stiff", mine, other, other_half, near_stiff
    )
    kept, sent = pl.pallas_call(
        final_body,
        out_shape=[jax.ShapeDtypeStruct((128, 1024), F32), jax.ShapeDtypeStruct((128, 1024), BF16)],
        in_specs=[VM] * 4,
        out_specs=[VM, VM],
        scratch_shapes=[pltpu.VMEM((256, 1024), F32)],
        compiler_params=pltpu.CompilerParams(vmem_limit_bytes=12 << 20),
        cost_estimate=pl.CostEstimate(flops=0, bytes_accessed=0, transcendentals=0),
        name="product",
    )(stiff, modes, right, columns)
    total = (kept + swap(sent, "c", 1).astype(F32)).astype(BF16)
    pieces = exchange(total.reshape(16, 8, 1024), ("z", "x"))
    return jnp.sum(pieces.astype(F32), axis=0)[None]


def solution(mesh):
    names = ("g", "b", "a", "z", "x", "c")
    split = Mesh(mesh.devices.reshape(4, 2, 2, 4, 4, 2), names)
    leaf = ("g", "b", "a")
    placed = (
        P(leaf, None, PANEL),
        P(leaf, PANEL, None),
        P(leaf, None, None),
        P(leaf, None),
        P(leaf, None),
        P(leaf, PANEL, None),
        P(leaf, None, None),
        P(leaf, None),
        P(),
        P(leaf, PANEL, None),
    )
    return jax.shard_map(
        shards, mesh=split, in_specs=placed, out_specs=P(leaf, PANEL, None), check_vma=False
    )
```
